32 devices in a mesh: dp: 8 (over y, x, core), tensor: 4 (over z).
Axes of the slice: x: 2, y: 2, z: 4, core: 2. Of those that a mesh axis runs over, the one named last changes fastest.
Arguments:
- tokens: bfloat16 [13056, 1024], P(('dp', 'tensor')), may hold values from -6 to 6
- lengths: int32 [25], replicated, may hold values from 32 to 1024, as said below
- gain_attn: float32 [1024], replicated, may hold values from 0.1 to 1.9
- w_qkv: bfloat16 [1024, 3, 1024], P(None, None, 'tensor'), may hold values from -0.1875 to 0.1875
- w_out: bfloat16 [1024, 1024], P('tensor'), may hold values from -1 to 1
- gain_ffn: float32 [1024], replicated, may hold values from 0.1 to 1.9
- w_in: bfloat16 [1024, 2, 2624], P(None, None, 'tensor'), may hold values from -0.1875 to 0.1875
- w_down: bfloat16 [2624, 1024], P('tensor'), may hold values from -0.15625 to 0.15625
- grad_output: bfloat16 [13056, 1024], P(('dp', 'tensor')), may hold values from -8 to 8
Outputs:
- output: bfloat16 [13056, 1024], P(('dp', 'tensor'))
- grad_tokens: bfloat16 [13056, 1024], P(('dp', 'tensor'))
- grad_gain_attn: float32 [1024], replicated
- grad_w_qkv: float32 [1024, 3, 1024], P('dp', None, 'tensor')
- grad_w_out: float32 [1024, 1024], P('tensor', 'dp')
- grad_gain_ffn: float32 [1024], replicated
- grad_w_in: float32 [1024, 2, 2624], P('dp', None, 'tensor')
- grad_w_down: float32 [2624, 1024], P('tensor', 'dp')
The draws below stay inside these ranges and needn't reach their ends.
Inputs may be any that keep to these rules, and one draw needn't show every extreme that they name: The lengths sum to 13056. Document 0 starts at token 0; besides it, each aligned block of 544 tokens that starts at a multiple of 544 holds exactly one document start, at least 32 tokens after the run's first token and at most 512 after it.
All inputs are finite; a program needn't handle non-finite values.
Results may differ from the reference program's by a relative error of at most 0.024.
Values may be sent and summed in bfloat16 or wider, within the bound.
A program may use at most 128 MiB of HBM per device.

```python
import math
import jax
import jax.numpy as jnp
from jax import lax

D = 1024
HEADS = 16
HD = 64
FF = 2624
HALF = 64
SPAN = 544
EDGE = 32
TOKENS = 13056


def draw_lengths(key, part):
    key = jax.random.fold_in(key, 7)
    amount = TOKENS // SPAN
    key_offsets, key_chosen = jax.random.split(key)
    offsets = jax.random.randint(key_offsets, (amount,), EDGE, SPAN - EDGE + 1)
    chosen = jax.random.randint(key_chosen, (), 0, amount - 1)
    index = jnp.arange(amount, dtype=jnp.int32)
    offsets = jnp.where(index == chosen, EDGE, offsets)
    offsets = jnp.where(index == chosen + 1, SPAN - EDGE, offsets)
    starts = index * SPAN + offsets
    bounds = jnp.concatenate([jnp.zeros((1,), jnp.int32), starts.astype(jnp.int32), jnp.full((1,), TOKENS, jnp.int32)])
    return (bounds[1:] - bounds[:-1]).astype(jnp.int32)


def draw_grad_output(key, part):
    key = jax.random.fold_in(key, 11)
    ladder = jnp.arange(TOKENS, dtype=jnp.float32)[:, None] / TOKENS
    values = jnp.clip(jax.random.normal(key, (TOKENS, D), jnp.float32), -5.0, 5.0) * (0.5 + ladder)
    return values.astype(jnp.bfloat16)


def level_of(own_key, dims, shards, least, high):
    loudness, own = 1.0, jax.random.fold_in(own_key, 6)
    for position, parts in shards:
        draws = jnp.exp(jax.random.uniform(jax.random.fold_in(own, position), (parts,), jnp.float32, least / len(shards), high / len(shards)))
        loudness = loudness * jnp.repeat(draws, dims[position] // parts).reshape([-1 if axis == position else 1 for axis in range(len(dims))])
    return loudness


def centred(rng, extent, scale, limit, cuts=(), kind=jnp.bfloat16):
    drawn = scale * jax.random.normal(rng, extent, jnp.float32)
    if cuts:
        drawn = drawn * level_of(rng, extent, cuts, -0.22, 0.18)
    return jnp.clip(drawn, -limit, limit).astype(kind)


def setup_inputs(seed: int = 0) -> dict:
    streams_of = jax.random.split(jax.random.key(seed), 10)
    tokens = centred(streams_of[0], (TOKENS, D), 1.0, 6.0, ((0, 32),))
    lengths = draw_lengths(jax.random.fold_in(streams_of[9], 71), 0)
    gain_attn = jnp.clip(1.0 + 0.18 * jax.random.normal(streams_of[2], (D,), jnp.float32), 0.1, 1.9)
    w_qkv = centred(streams_of[3], (D, 3, HEADS * HD), D ** -0.5, 0.1875, ((2, 4),))
    w_out = centred(streams_of[4], (HEADS * HD, D), (HEADS * HD // 32) ** -0.5, 1.0, ((0, 4),))
    gain_ffn = jnp.clip(1.0 + 0.18 * jax.random.normal(streams_of[5], (D,), jnp.float32), 0.1, 1.9)
    w_in = centred(streams_of[6], (D, 2, FF), D ** -0.5, 0.1875, ((2, 4),))
    w_down = centred(streams_of[7], (FF, D), (FF // 2) ** -0.5, 0.15625, ((0, 4),))
    grad_output = draw_grad_output(jax.random.fold_in(streams_of[9], 71), 0)
    return {"tokens": tokens, "lengths": lengths, "gain_attn": gain_attn, "w_qkv": w_qkv, "w_out": w_out, "gain_ffn": gain_ffn, "w_in": w_in, "w_down": w_down, "grad_output": grad_output}


EPS = 1e-05
THETA = 10000.0
HIGHEST = lax.Precision.HIGHEST

@jax.custom_vjp
def low(v):
    return lax.optimization_barrier(v.astype(jnp.bfloat16)).astype(jnp.float32)

@jax.custom_vjp
def low_back(v):
    return v

def low_keep(v):
    return (low(v), None)

def low_pass(kept, grad):
    return (grad,)

def back_keep(v):
    return (v, None)

def back_low(kept, grad):
    return (low(grad),)
low.defvjp(low_keep, low_pass)
low_back.defvjp(back_keep, back_low)

def layer_norm(values, gain_vec):
    center = values - lax.optimization_barrier(jnp.mean(values, axis=-1, keepdims=True))
    spread = lax.optimization_barrier(jnp.mean(center * center, axis=-1, keepdims=True))
    return center * lax.rsqrt(spread + EPS) * gain_vec

def layout(lengths, first, amount, total):
    places = first + jnp.arange(amount, dtype=jnp.int32)
    cuts = jnp.cumsum(lengths)[:-1].astype(jnp.int32)
    before = cuts[None, :] <= places[:, None]
    doc_ids = lax.optimization_barrier(jnp.sum(before.astype(jnp.int32), axis=1)).astype(jnp.int32)
    begins = lax.optimization_barrier(jnp.max(jnp.where(before, cuts[None, :], 0), axis=1)).astype(jnp.int32)
    positions = places - begins
    valid = (places >= 0) & (places < total)
    return (jnp.where(valid, doc_ids, -1).astype(jnp.int32), positions)

def rotary(positions):
    half_dim = HD // 2
    inverse = jnp.exp(jnp.arange(half_dim, dtype=jnp.float32) * (-2.0 * math.log(THETA) / HD))
    angles = positions.astype(jnp.float32)[:, None] * inverse[None, :]
    return (jnp.cos(angles)[:, None, :], jnp.sin(angles)[:, None, :])

def rotate(values, cosine, sine):
    half_dim = values.shape[-1] // 2
    first_half = values[..., :half_dim]
    second_half = values[..., half_dim:]
    return jnp.concatenate([first_half * cosine - second_half * sine, second_half * cosine + first_half * sine], axis=-1)

def gelu_product(hidden):
    return jax.nn.gelu(hidden[:, 0], approximate=False) * hidden[:, 1]

def attend(queries, keys, values, doc_ids):
    factor = 1.0 / math.sqrt(HD)
    keys_pad = jnp.pad(keys, ((HALF, HALF), (0, 0), (0, 0)))
    values_pad = jnp.pad(values, ((HALF, HALF), (0, 0), (0, 0)))
    seg_pad = jnp.pad(doc_ids, (HALF, HALF), constant_values=-1)

    def one_block(number):
        offset = (number * SPAN).astype(jnp.int32)
        query_part = lax.dynamic_slice_in_dim(queries, offset, SPAN, 0)
        key_part = lax.dynamic_slice_in_dim(keys_pad, offset, SPAN + 2 * HALF, 0)
        value_part = lax.dynamic_slice_in_dim(values_pad, offset, SPAN + 2 * HALF, 0)
        seg_query = lax.dynamic_slice_in_dim(doc_ids, offset, SPAN, 0)
        seg_key = lax.dynamic_slice_in_dim(seg_pad, offset, SPAN + 2 * HALF, 0)
        row_ids = jnp.arange(SPAN, dtype=jnp.int32)[:, None]
        col_ids = jnp.arange(SPAN + 2 * HALF, dtype=jnp.int32)[None, :]
        allowed = (jnp.abs(col_ids - HALF - row_ids) <= HALF) & (seg_query[:, None] == seg_key[None, :])
        scores = low_back(jnp.einsum('qhd,khd->hqk', query_part, key_part, precision=HIGHEST) * factor)
        probs = jax.nn.softmax(jnp.where(allowed[None], scores, -1e+30), axis=-1)
        return jnp.einsum('hqk,khd->qhd', low(probs), value_part, precision=HIGHEST)
    mixed = lax.map(jax.checkpoint(one_block), jnp.arange(TOKENS // SPAN, dtype=jnp.int32))
    return mixed.reshape(TOKENS, HEADS * HD)

def reference(tokens, lengths, gain_attn, w_qkv, w_out, gain_ffn, w_in, w_down, grad_output):
    doc_ids, positions = layout(lengths, 0, TOKENS, TOKENS)
    cosine, sine = rotary(positions)

    def forward(inputs, gain_one, weight_qkv, weight_out, gain_two, weight_in, weight_down):
        normed = low(layer_norm(inputs, gain_one))
        projected = low_back(jnp.dot(normed, weight_qkv.reshape(D, 3 * HEADS * HD), precision=HIGHEST, preferred_element_type=jnp.float32))
        projected = projected.reshape(TOKENS, 3, HEADS, HD)
        queries = low(rotate(projected[:, 0], cosine, sine))
        keys = low(rotate(projected[:, 1], cosine, sine))
        values = low(projected[:, 2])
        mixed = low(low_back(attend(queries, keys, values, doc_ids)))
        residual = inputs + low_back(jnp.dot(mixed, weight_out, precision=HIGHEST, preferred_element_type=jnp.float32))
        normed_ffn = low(layer_norm(residual, gain_two))
        hidden = low_back(jnp.dot(normed_ffn, weight_in.reshape(D, 2 * FF), precision=HIGHEST, preferred_element_type=jnp.float32))
        activated = low(gelu_product(hidden.reshape(TOKENS, 2, FF)))
        return residual + low_back(jnp.dot(activated, weight_down, precision=HIGHEST, preferred_element_type=jnp.float32))
    result, pullback = jax.vjp(forward, tokens.astype(jnp.float32), gain_attn.astype(jnp.float32), w_qkv.astype(jnp.float32), w_out.astype(jnp.float32), gain_ffn.astype(jnp.float32), w_in.astype(jnp.float32), w_down.astype(jnp.float32))
    grads = pullback(grad_output.astype(jnp.float32))
    return (result.astype(jnp.bfloat16), grads[0].astype(jnp.bfloat16), grads[1], grads[2], grads[3], grads[4], grads[5], grads[6])
```

```python
import math

import jax
import jax.numpy as jnp
from jax import lax
from jax.experimental import pallas as pl
from jax.experimental.pallas import tpu as pltpu
from jax.sharding import PartitionSpec as P

D = 1024
HD = 64
HALF = 64
LANES = 128
EPS = 1e-05
THETA = 10000.0
ROWS = ("dp", "tensor")
PIECES = ("tensor", "dp")
BF = jnp.bfloat16
F32 = jnp.float32


def layer_norm(values, gain_vec):
    center = values - jnp.mean(values, axis=-1, keepdims=True)
    spread = jnp.mean(center * center, axis=-1, keepdims=True)
    return center * lax.rsqrt(spread + EPS) * gain_vec


def layout(lengths, first, amount, total):
    places = first + jnp.arange(amount, dtype=jnp.int32)
    cuts = jnp.cumsum(lengths)[:-1]
    before = cuts[None, :] <= places[:, None]
    doc_ids = jnp.sum(before.astype(jnp.int32), axis=1)
    begins = jnp.max(jnp.where(before, cuts[None, :], 0), axis=1)
    positions = places - begins
    valid = (places >= 0) & (places < total)
    return (jnp.where(valid, doc_ids, -1), positions)


def rotary(positions):
    half_dim = HD // 2
    inverse = jnp.exp(jnp.arange(half_dim, dtype=F32) * (-2.0 * math.log(THETA) / HD))
    angles = positions.astype(F32)[:, None] * inverse[None, :]
    cosine, sine = jnp.cos(angles), jnp.sin(angles)
    return (
        jnp.concatenate([cosine] * 4, axis=1),
        jnp.concatenate([-sine, sine, -sine, sine], axis=1),
    )


def dot(a, b, dims):
    return lax.dot_general(a, b, (dims, ((), ())), preferred_element_type=F32)


NT = ((1,), (1,))
NN = ((1,), (0,))
TN = ((0,), (0,))


def swap(u):
    lane = lax.broadcasted_iota(jnp.int32, u.shape, 1)
    return jnp.where((lane & 32) == 0, pltpu.roll(u, 96, 1), pltpu.roll(u, 32, 1))


def cut_blocks(rows):
    count = max(rows // LANES, 1)
    return [
        (i * LANES, LANES if i < count - 1 else rows - (count - 1) * LANES) for i in range(count)
    ]


def head_masks(rows):
    lane = lax.broadcasted_iota(jnp.int32, (rows, LANES), 1)
    return ((lane < HD).astype(F32), (lane >= HD).astype(F32))


def load_qkv(rows, q_ref, k_ref, v_ref, c_ref, s_ref):
    cosine, sine = c_ref[...], s_ref[...]
    q = q_ref[0, HALF : HALF + rows, :]
    q = q * cosine[HALF : HALF + rows] + swap(q) * sine[HALF : HALF + rows]
    q = q.astype(BF).astype(F32) * (1.0 / math.sqrt(HD))
    k = k_ref[0]
    k = (k * cosine + swap(k) * sine).astype(BF)
    return q, k, v_ref[0].astype(BF), cosine, sine


def soft(qh, kw, bias):
    scores = dot(qh, kw, NT) + bias
    raised = jnp.exp(scores - jnp.max(scores, axis=1, keepdims=True))
    return raised * (1.0 / jnp.sum(raised, axis=1, keepdims=True))


def fwd_kernel(rows, q_ref, k_ref, v_ref, c_ref, s_ref, b_ref, o_ref):
    q, k, v, _, _ = load_qkv(rows, q_ref, k_ref, v_ref, c_ref, s_ref)
    parts = []
    for start, size in cut_blocks(rows):
        stop = start + size + 2 * HALF
        kw, vw = k[start:stop], v[start:stop]
        bias = b_ref[start : start + size, start:stop]
        masks = head_masks(size)
        total = None
        for mask in masks:
            qh = (q[start : start + size] * mask).astype(BF)
            p = soft(qh, kw, bias)
            part = dot(p.astype(BF), vw, NN) * mask
            total = part if total is None else total + part
        parts.append(total)
    o_ref[0] = jnp.concatenate(parts, axis=0).astype(BF)


def bwd_kernel(rows, q_ref, k_ref, v_ref, c_ref, s_ref, b_ref, g_ref, o_ref, acc):
    which = pl.program_id(1)

    @pl.when(which == 0)
    def _():
        q, k, v, cosine, sine = load_qkv(rows, q_ref, k_ref, v_ref, c_ref, s_ref)
        g = g_ref[0].astype(F32)
        acc[...] = jnp.zeros_like(acc)
        for start, size in cut_blocks(rows):
            stop = start + size + 2 * HALF
            kw, vw = k[start:stop], v[start:stop]
            bias = b_ref[start : start + size, start:stop]
            dq = None
            for mask in head_masks(size):
                qh = (q[start : start + size] * mask).astype(BF)
                gh = (g[start : start + size] * mask).astype(BF)
                p = soft(qh, kw, bias)
                dp = dot(gh, vw, NT)
                centre = jnp.sum(p * dp, axis=1, keepdims=True)
                ds = (p * (dp - centre)).astype(BF)
                part = dot(ds, kw, NN) * (mask * (1.0 / math.sqrt(HD)))
                dq = part if dq is None else dq + part
                acc[1, start:stop, :] += dot(ds, qh, TN)
                acc[2, start:stop, :] += dot(p.astype(BF), gh, TN)
            acc[0, HALF + start : HALF + start + size, :] = dq
        for index in range(2):
            w = acc[index]
            acc[index] = w * cosine - swap(w) * sine

    o_ref[0] = acc[which].astype(BF)


def attention_specs(rows, ext, per):
    def column(j):
        return pl.BlockSpec((1, ext, LANES), lambda i, *_: (i // per, 0, j * per + i % per))

    whole = pl.BlockSpec((ext, LANES), lambda *_: (0, 0))
    bias = pl.BlockSpec((rows, ext), lambda *_: (0, 0))
    return [column(0), column(1), column(2), whole, whole, bias]


def attend_fwd(rows, projected, cosine, sine, bias):
    tp, ext, width = projected.shape
    per = width // 3 // LANES
    return pl.pallas_call(
        lambda *refs: fwd_kernel(rows, *refs),
        grid=(tp * per,),
        in_specs=attention_specs(rows, ext, per),
        out_specs=pl.BlockSpec((1, rows, LANES), lambda i: (i // per, 0, i % per)),
        out_shape=jax.ShapeDtypeStruct((tp, rows, width // 3), BF),
        compiler_params=pltpu.CompilerParams(vmem_limit_bytes=32 * 1024 * 1024),
    )(projected, projected, projected, cosine, sine, bias)


def attend_bwd(rows, projected, cosine, sine, bias, grad):
    tp, ext, width = projected.shape
    per = width // 3 // LANES
    specs = attention_specs(rows, ext, per)
    specs.append(pl.BlockSpec((1, rows, LANES), lambda i, j: (i // per, 0, i % per)))
    return pl.pallas_call(
        lambda *refs: bwd_kernel(rows, *refs),
        grid=(tp * per, 3),
        in_specs=specs,
        out_specs=pl.BlockSpec((1, ext, LANES), lambda i, j: (i // per, 0, j * per + i % per)),
        out_shape=jax.ShapeDtypeStruct((tp, ext, width), BF),
        scratch_shapes=[pltpu.VMEM((3, ext, LANES), F32)],
        compiler_params=pltpu.CompilerParams(vmem_limit_bytes=32 * 1024 * 1024),
    )(projected, projected, projected, cosine, sine, bias, grad)


def total_over_all(value):
    for axis in ROWS:
        count, step = lax.axis_size(axis), 1
        while step < count:
            value = value + lax.ppermute(value, axis, [(i, i ^ step) for i in range(count)])
            step *= 2
    return value


def ein(spec, a, b):
    return jnp.einsum(spec, a, b, preferred_element_type=F32)


def body(tokens, lengths, gain_attn, w_qkv, w_out, gain_ffn, w_in, w_down, grad_output):
    rows = tokens.shape[0]
    dp, tp = lax.axis_size("dp"), lax.axis_size("tensor")
    devices = dp * tp
    total = rows * devices
    ext = rows + 2 * HALF
    deep = D // dp
    first = lax.axis_index("dp") * deep
    heads_width, units = w_qkv.shape[2], w_in.shape[2]

    piece = jnp.concatenate(
        [
            lax.dynamic_slice_in_dim(w_qkv, first, deep, 0).reshape(deep, 3 * heads_width),
            lax.dynamic_slice_in_dim(w_out, first, deep, 1).T,
            lax.dynamic_slice_in_dim(w_in, first, deep, 0).reshape(deep, 2 * units),
            lax.dynamic_slice_in_dim(w_down, first, deep, 1).T,
        ],
        axis=1,
    )
    gathered = lax.all_gather(piece, PIECES, axis=0, tiled=True).reshape(tp, D, -1)
    edges = [0, 3 * heads_width, 4 * heads_width, 4 * heads_width + 2 * units]
    edges.append(edges[-1] + units)
    all_qkv, all_out, all_in, all_down = (
        gathered[:, :, edges[i] : edges[i + 1]] for i in range(4)
    )

    start = (lax.axis_index("dp") * tp + lax.axis_index("tensor")) * rows
    forward = [(i, i + 1) for i in range(devices - 1)]
    backward = [(i + 1, i) for i in range(devices - 1)]
    x_own = tokens.astype(F32)
    normed_own, norm_pull_one = jax.vjp(layer_norm, x_own, gain_attn)
    normed_low = normed_own.astype(BF)
    normed_ext = jnp.concatenate(
        [
            lax.ppermute(normed_low[rows - HALF :], ROWS, forward),
            normed_low,
            lax.ppermute(normed_low[:HALF], ROWS, backward),
        ],
        axis=0,
    )
    seg_ext, pos_ext = layout(lengths, start - HALF, ext, total)
    cosine, sine = rotary(pos_ext)
    row_ids = jnp.arange(rows, dtype=jnp.int32)[:, None]
    col_ids = jnp.arange(ext, dtype=jnp.int32)[None, :]
    allowed = (jnp.abs(col_ids - HALF - row_ids) <= HALF) & (
        seg_ext[HALF : HALF + rows][:, None] == seg_ext[None, :]
    )
    bias = jnp.where(allowed, 0.0, -1e30).astype(F32)

    projected = ein("nd,tdk->tnk", normed_ext, all_qkv)
    mixed = attend_fwd(rows, projected, cosine, sine, bias)
    residual = x_own + ein("tnc,tdc->nd", mixed, all_out)
    normed_ffn, norm_pull_two = jax.vjp(layer_norm, residual, gain_ffn)
    normed_ffn_low = normed_ffn.astype(BF)
    hidden = ein("nd,tdk->tnk", normed_ffn_low, all_in)

    def gelu_product(values):
        return jax.nn.gelu(values[..., :units], approximate=False) * values[..., units:]

    activated, gelu_pull = jax.vjp(gelu_product, hidden)
    act_low = activated.astype(BF)
    output = (residual + ein("tnf,tdf->nd", act_low, all_down)).astype(BF)

    grad_out32 = grad_output.astype(F32)
    grad_act = ein("nd,tdf->tnf", grad_output, all_down)
    grad_hidden = gelu_pull(grad_act)[0].astype(BF)
    grad_down = ein("nd,tnf->tdf", grad_output, act_low).astype(BF)
    grad_in = ein("nd,tnk->tdk", normed_ffn_low, grad_hidden).astype(BF)
    ffn_sum = lax.psum_scatter(
        jnp.concatenate([grad_in, grad_down], axis=2).reshape(tp * D, 3 * units),
        PIECES,
        scatter_dimension=0,
        tiled=True,
    )
    grad_normed_ffn = ein("tnk,tdk->nd", grad_hidden, all_in)
    grad_resid_part, grad_gain_two = norm_pull_two(grad_normed_ffn)
    grad_residual = grad_out32 + grad_resid_part
    grad_res_low = grad_residual.astype(BF)
    grad_mixed = ein("nd,tdc->tnc", grad_res_low, all_out).astype(BF)
    grad_wout = ein("nd,tnc->tdc", grad_res_low, mixed).astype(BF)
    grad_qkv_low = attend_bwd(rows, projected, cosine, sine, bias, grad_mixed)
    grad_wqkv = ein("nd,tnk->tdk", normed_ext, grad_qkv_low).astype(BF)
    attn_sum = lax.psum_scatter(
        jnp.concatenate([grad_wqkv, grad_wout], axis=2).reshape(tp * D, 4 * heads_width),
        PIECES,
        scatter_dimension=0,
        tiled=True,
    )
    grad_normed_ext = ein("tnk,tdk->nd", grad_qkv_low, all_qkv)
    from_after = lax.ppermute(grad_normed_ext[:HALF].astype(BF), ROWS, backward)
    from_before = lax.ppermute(grad_normed_ext[ext - HALF :].astype(BF), ROWS, forward)
    grad_normed = (
        grad_normed_ext[HALF : HALF + rows]
        + jnp.pad(from_before.astype(F32), ((0, rows - HALF), (0, 0)))
        + jnp.pad(from_after.astype(F32), ((rows - HALF, 0), (0, 0)))
    )
    grad_x_part, grad_gain_one = norm_pull_one(grad_normed)
    grad_tokens = (grad_residual + grad_x_part).astype(BF)
    gains = total_over_all(jnp.stack([grad_gain_one, grad_gain_two]))

    ffn_sum = ffn_sum.astype(F32)
    attn_sum = attn_sum.astype(F32)
    return (
        output,
        grad_tokens,
        gains[0],
        attn_sum[:, : 3 * heads_width].reshape(deep, 3, heads_width),
        attn_sum[:, 3 * heads_width :].T,
        gains[1],
        ffn_sum[:, : 2 * units].reshape(deep, 2, units),
        ffn_sum[:, 2 * units :].T,
    )


def solution(mesh):
    in_specs = (
        P(("dp", "tensor"), None),
        P(),
        P(),
        P(None, None, "tensor"),
        P("tensor", None),
        P(),
        P(None, None, "tensor"),
        P("tensor", None),
        P(("dp", "tensor"), None),
    )
    out_specs = (
        P(("dp", "tensor"), None),
        P(("dp", "tensor"), None),
        P(),
        P("dp", None, "tensor"),
        P("tensor", "dp"),
        P(),
        P("dp", None, "tensor"),
        P("tensor", "dp"),
    )
    return jax.shard_map(body, mesh=mesh, in_specs=in_specs, out_specs=out_specs, check_vma=False)
```

```python
import math

import jax
import jax.numpy as jnp
from jax import lax
from jax.experimental import pallas as pl
from jax.experimental.pallas import tpu as pltpu
from jax.experimental.layout import Layout, with_layout_constraint
from jax.sharding import PartitionSpec as P

D = 1024
HD = 64
HALF = 64
LANES = 128
EPS = 1e-05
THETA = 10000.0
ROWS = ("dp", "tensor")
PIECES = ("tensor", "dp")
BF = jnp.bfloat16
F32 = jnp.float32


def layer_norm(values, gain_vec):
    center = values - jnp.mean(values, axis=-1, keepdims=True)
    spread = jnp.mean(center * center, axis=-1, keepdims=True)
    return center * lax.rsqrt(spread + EPS) * gain_vec


def layout(lengths, first, amount, total):
    places = first + jnp.arange(amount, dtype=jnp.int32)
    cuts = jnp.cumsum(lengths)[:-1]
    before = cuts[None, :] <= places[:, None]
    doc_ids = jnp.sum(before.astype(jnp.int32), axis=1)
    begins = jnp.max(jnp.where(before, cuts[None, :], 0), axis=1)
    positions = places - begins
    valid = (places >= 0) & (places < total)
    return (jnp.where(valid, doc_ids, -1), positions)


def rotary(positions):
    half_dim = HD // 2
    inverse = jnp.exp(jnp.arange(half_dim, dtype=F32) * (-2.0 * math.log(THETA) / HD))
    angles = positions.astype(F32)[:, None] * inverse[None, :]
    cosine, sine = jnp.cos(angles), jnp.sin(angles)
    return (
        jnp.concatenate([cosine] * 4, axis=1),
        jnp.concatenate([-sine, sine, -sine, sine], axis=1),
    )


def dot(a, b, dims):
    return lax.dot_general(a, b, (dims, ((), ())), preferred_element_type=F32)


NT = ((1,), (1,))
NN = ((1,), (0,))
TN = ((0,), (0,))


def swap(u):
    lane = lax.broadcasted_iota(jnp.int32, u.shape, 1)
    return jnp.where((lane & 32) == 0, pltpu.roll(u, 96, 1), pltpu.roll(u, 32, 1))


def cut_blocks(rows):
    count = max(rows // LANES, 1)
    return [
        (i * LANES, LANES if i < count - 1 else rows - (count - 1) * LANES) for i in range(count)
    ]


def head_masks(rows):
    lane = lax.broadcasted_iota(jnp.int32, (rows, LANES), 1)
    return ((lane < HD).astype(F32), (lane >= HD).astype(F32))


def load_qkv(rows, q_ref, k_ref, v_ref, c_ref, s_ref):
    cosine, sine = c_ref[...], s_ref[...]
    q = q_ref[0, HALF : HALF + rows, :]
    q = q * cosine[HALF : HALF + rows] + swap(q) * sine[HALF : HALF + rows]
    q = q.astype(BF).astype(F32) * (1.0 / math.sqrt(HD))
    k = k_ref[0]
    k = (k * cosine + swap(k) * sine).astype(BF)
    return q, k, v_ref[0].astype(BF), cosine, sine


def soft(qh, kw, bias):
    scores = dot(qh, kw, NT) + bias
    raised = jnp.exp(scores - jnp.max(scores, axis=1, keepdims=True))
    return raised * (1.0 / jnp.sum(raised, axis=1, keepdims=True))


def fwd_kernel(rows, q_ref, k_ref, v_ref, c_ref, s_ref, b_ref, o_ref):
    q, k, v, _, _ = load_qkv(rows, q_ref, k_ref, v_ref, c_ref, s_ref)
    parts = []
    for start, size in cut_blocks(rows):
        stop = start + size + 2 * HALF
        kw, vw = k[start:stop], v[start:stop]
        bias = b_ref[start : start + size, start:stop]
        masks = head_masks(size)
        total = None
        for mask in masks:
            qh = (q[start : start + size] * mask).astype(BF)
            p = soft(qh, kw, bias)
            part = dot(p.astype(BF), vw, NN) * mask
            total = part if total is None else total + part
        parts.append(total)
    o_ref[0] = jnp.concatenate(parts, axis=0).astype(BF)


def bwd_kernel(rows, q_ref, k_ref, v_ref, c_ref, s_ref, b_ref, g_ref, o_ref, acc):
    which = pl.program_id(1)

    @pl.when(which == 0)
    def _():
        q, k, v, cosine, sine = load_qkv(rows, q_ref, k_ref, v_ref, c_ref, s_ref)
        g = g_ref[0].astype(F32)
        acc[...] = jnp.zeros_like(acc)
        for start, size in cut_blocks(rows):
            stop = start + size + 2 * HALF
            kw, vw = k[start:stop], v[start:stop]
            bias = b_ref[start : start + size, start:stop]
            dq = None
            for mask in head_masks(size):
                qh = (q[start : start + size] * mask).astype(BF)
                gh = (g[start : start + size] * mask).astype(BF)
                p = soft(qh, kw, bias)
                dp = dot(gh, vw, NT)
                centre = jnp.sum(p * dp, axis=1, keepdims=True)
                ds = (p * (dp - centre)).astype(BF)
                part = dot(ds, kw, NN) * (mask * (1.0 / math.sqrt(HD)))
                dq = part if dq is None else dq + part
                acc[1, start:stop, :] += dot(ds, qh, TN)
                acc[2, start:stop, :] += dot(p.astype(BF), gh, TN)
            acc[0, HALF + start : HALF + start + size, :] = dq
        for index in range(2):
            w = acc[index]
            acc[index] = w * cosine - swap(w) * sine

    o_ref[0] = acc[which].astype(BF)


def attention_specs(rows, ext, per):
    def column(j):
        return pl.BlockSpec((1, ext, LANES), lambda i, *_: (i // per, 0, j * per + i % per))

    whole = pl.BlockSpec((ext, LANES), lambda *_: (0, 0))
    bias = pl.BlockSpec((rows, ext), lambda *_: (0, 0))
    return [column(0), column(1), column(2), whole, whole, bias]


def attend_fwd(rows, projected, cosine, sine, bias):
    tp, ext, width = projected.shape
    per = width // 3 // LANES
    return pl.pallas_call(
        lambda *refs: fwd_kernel(rows, *refs),
        grid=(tp * per,),
        in_specs=attention_specs(rows, ext, per),
        out_specs=pl.BlockSpec((1, rows, LANES), lambda i: (i // per, 0, i % per)),
        out_shape=jax.ShapeDtypeStruct((tp, rows, width // 3), BF),
        compiler_params=pltpu.CompilerParams(vmem_limit_bytes=32 * 1024 * 1024),
    )(projected, projected, projected, cosine, sine, bias)


def attend_bwd(rows, projected, cosine, sine, bias, grad):
    tp, ext, width = projected.shape
    per = width // 3 // LANES
    specs = attention_specs(rows, ext, per)
    specs.append(pl.BlockSpec((1, rows, LANES), lambda i, j: (i // per, 0, i % per)))
    return pl.pallas_call(
        lambda *refs: bwd_kernel(rows, *refs),
        grid=(tp * per, 3),
        in_specs=specs,
        out_specs=pl.BlockSpec((1, ext, LANES), lambda i, j: (i // per, 0, j * per + i % per)),
        out_shape=jax.ShapeDtypeStruct((tp, ext, width), BF),
        scratch_shapes=[pltpu.VMEM((3, ext, LANES), F32)],
        compiler_params=pltpu.CompilerParams(vmem_limit_bytes=32 * 1024 * 1024),
    )(projected, projected, projected, cosine, sine, bias, grad)


def pair_kernel(l1_ref, r1_ref, l2_ref, r2_ref, o_ref):
    width = r1_ref.shape[2]
    o_ref[:, :width] = dot(l1_ref[...], r1_ref[0], TN).astype(BF)
    o_ref[:, width:] = dot(l2_ref[...], r2_ref[0], TN).astype(BF)


def pair_products(l1, r1, l2, r2):
    tp, n1, k1 = r1.shape
    n2, k2 = r2.shape[1:]
    deep = l1.shape[1]
    tile = 2 * LANES
    count = deep // tile
    return pl.pallas_call(
        pair_kernel,
        grid=(tp, count),
        in_specs=[
            pl.BlockSpec((n1, tile), lambda t, j: (0, j)),
            pl.BlockSpec((1, n1, k1), lambda t, j: (t, 0, 0)),
            pl.BlockSpec((n2, tile), lambda t, j: (0, j)),
            pl.BlockSpec((1, n2, k2), lambda t, j: (t, 0, 0)),
        ],
        out_specs=pl.BlockSpec((tile, k1 + k2), lambda t, j: (t * count + j, 0)),
        out_shape=jax.ShapeDtypeStruct((tp * deep, k1 + k2), BF),
        compiler_params=pltpu.CompilerParams(vmem_limit_bytes=32 * 1024 * 1024),
    )(l1, r1, l2, r2)


def padded(block):
    return jnp.pad(block, ((0, 0), (0, -block.shape[1] % LANES)))


def total_over_all(value):
    for axis in ROWS:
        count, step = lax.axis_size(axis), 1
        while step < count:
            value = value + lax.ppermute(value, axis, [(i, i ^ step) for i in range(count)])
            step *= 2
    return value


def ein(spec, a, b):
    return jnp.einsum(spec, a, b, preferred_element_type=F32)


def body(tokens, lengths, gain_attn, w_qkv, w_out, gain_ffn, w_in, w_down, grad_output):
    rows = tokens.shape[0]
    dp, tp = lax.axis_size("dp"), lax.axis_size("tensor")
    devices = dp * tp
    total = rows * devices
    ext = rows + 2 * HALF
    deep = D // dp
    first = lax.axis_index("dp") * deep
    heads_width, units = w_qkv.shape[2], w_in.shape[2]

    blocks = [
        lax.dynamic_slice_in_dim(w_qkv, first, deep, 0).reshape(deep, 3 * heads_width),
        lax.dynamic_slice_in_dim(w_out, first, deep, 1).T,
        lax.dynamic_slice_in_dim(w_in, first, deep, 0).reshape(deep, 2 * units),
        lax.dynamic_slice_in_dim(w_down, first, deep, 1).T,
    ]
    piece = jnp.concatenate([padded(block) for block in blocks], axis=1)
    gathered = lax.all_gather(piece, PIECES, axis=0, tiled=True)
    gathered = with_layout_constraint(gathered, Layout((0, 1))).reshape(tp, D, -1)
    weights, offset = [], 0
    for block in blocks:
        weights.append(gathered[:, :, offset : offset + block.shape[1]])
        offset += block.shape[1] + -block.shape[1] % LANES
    all_qkv, all_out, all_in, all_down = weights

    start = (lax.axis_index("dp") * tp + lax.axis_index("tensor")) * rows
    forward = [(i, i + 1) for i in range(devices - 1)]
    backward = [(i + 1, i) for i in range(devices - 1)]
    x_own = tokens.astype(F32)
    normed_own, norm_pull_one = jax.vjp(layer_norm, x_own, gain_attn)
    normed_low = normed_own.astype(BF)
    normed_ext = jnp.concatenate(
        [
            lax.ppermute(normed_low[rows - HALF :], ROWS, forward),
            normed_low,
            lax.ppermute(normed_low[:HALF], ROWS, backward),
        ],
        axis=0,
    )
    seg_ext, pos_ext = layout(lengths, start - HALF, ext, total)
    cosine, sine = rotary(pos_ext)
    row_ids = jnp.arange(rows, dtype=jnp.int32)[:, None]
    col_ids = jnp.arange(ext, dtype=jnp.int32)[None, :]
    allowed = (jnp.abs(col_ids - HALF - row_ids) <= HALF) & (
        seg_ext[HALF : HALF + rows][:, None] == seg_ext[None, :]
    )
    bias = jnp.where(allowed, 0.0, -1e30).astype(F32)

    projected = ein("nd,tdk->tnk", normed_ext, all_qkv)
    mixed = attend_fwd(rows, projected, cosine, sine, bias)
    residual = x_own + ein("tnc,tdc->nd", mixed, all_out)
    normed_ffn, norm_pull_two = jax.vjp(layer_norm, residual, gain_ffn)
    normed_ffn_low = normed_ffn.astype(BF)
    hidden = ein("nd,tdk->tnk", normed_ffn_low, all_in)

    def gelu_product(values):
        return jax.nn.gelu(values[..., :units], approximate=False) * values[..., units:]

    activated, gelu_pull = jax.vjp(gelu_product, hidden)
    act_low = activated.astype(BF)
    output = (residual + ein("tnf,tdf->nd", act_low, all_down)).astype(BF)

    grad_out32 = grad_output.astype(F32)
    grad_act = ein("nd,tdf->tnf", grad_output, all_down)
    grad_hidden = gelu_pull(grad_act)[0].astype(BF)
    ffn_terms = pair_products(normed_ffn_low, grad_hidden, grad_output, act_low)
    ffn_terms, grad_hidden = lax.optimization_barrier((ffn_terms, grad_hidden))
    ffn_sum = lax.psum_scatter(
        ffn_terms,
        PIECES,
        scatter_dimension=0,
        tiled=True,
    )
    grad_normed_ffn = ein("tnk,tdk->nd", grad_hidden, all_in)
    grad_resid_part, grad_gain_two = norm_pull_two(grad_normed_ffn)
    grad_residual = grad_out32 + grad_resid_part
    grad_res_low = grad_residual.astype(BF)
    grad_mixed = ein("nd,tdc->tnc", grad_res_low, all_out).astype(BF)
    grad_qkv_low = attend_bwd(rows, projected, cosine, sine, bias, grad_mixed)
    attn_terms = pair_products(normed_ext, grad_qkv_low, grad_res_low, mixed)
    attn_terms, ffn_sum = lax.optimization_barrier((attn_terms, ffn_sum))
    attn_sum = lax.psum_scatter(
        attn_terms,
        PIECES,
        scatter_dimension=0,
        tiled=True,
    )
    grad_normed_ext = ein("tnk,tdk->nd", grad_qkv_low, all_qkv)
    from_after = lax.ppermute(grad_normed_ext[:HALF].astype(BF), ROWS, backward)
    from_before = lax.ppermute(grad_normed_ext[ext - HALF :].astype(BF), ROWS, forward)
    grad_normed = (
        grad_normed_ext[HALF : HALF + rows]
        + jnp.pad(from_before.astype(F32), ((0, rows - HALF), (0, 0)))
        + jnp.pad(from_after.astype(F32), ((rows - HALF, 0), (0, 0)))
    )
    grad_x_part, grad_gain_one = norm_pull_one(grad_normed)
    grad_tokens = (grad_residual + grad_x_part).astype(BF)
    gains = total_over_all(jnp.stack([grad_gain_one, grad_gain_two]))

    ffn_sum = ffn_sum.astype(F32)
    attn_sum = attn_sum.astype(F32)
    return (
        output,
        grad_tokens,
        gains[0],
        attn_sum[:, : 3 * heads_width].reshape(deep, 3, heads_width),
        attn_sum[:, 3 * heads_width :].T,
        gains[1],
        ffn_sum[:, : 2 * units].reshape(deep, 2, units),
        ffn_sum[:, 2 * units :].T,
    )


def solution(mesh):
    in_specs = (
        P(("dp", "tensor"), None),
        P(),
        P(),
        P(None, None, "tensor"),
        P("tensor", None),
        P(),
        P(None, None, "tensor"),
        P("tensor", None),
        P(("dp", "tensor"), None),
    )
    out_specs = (
        P(("dp", "tensor"), None),
        P(("dp", "tensor"), None),
        P(),
        P("dp", None, "tensor"),
        P("tensor", "dp"),
        P(),
        P("dp", None, "tensor"),
        P("tensor", "dp"),
    )
    return jax.shard_map(body, mesh=mesh, in_specs=in_specs, out_specs=out_specs, check_vma=False)
```

```python
import math

import jax
import jax.numpy as jnp
from jax import lax
from jax.experimental import pallas as pl
from jax.experimental.pallas import tpu as pltpu
from jax.experimental.layout import Layout, with_layout_constraint
from jax.sharding import PartitionSpec as P

D = 1024
HD = 64
HALF = 64
LANES = 128
EPS = 1e-05
THETA = 10000.0
ROWS = ("dp", "tensor")
PIECES = ("tensor", "dp")
BF = jnp.bfloat16
F32 = jnp.float32


def layer_norm(values, gain_vec):
    center = values - jnp.mean(values, axis=-1, keepdims=True)
    spread = jnp.mean(center * center, axis=-1, keepdims=True)
    return center * lax.rsqrt(spread + EPS) * gain_vec


def layout(lengths, first, amount, total):
    places = first + jnp.arange(amount, dtype=jnp.int32)
    cuts = jnp.cumsum(lengths)[:-1]
    before = cuts[None, :] <= places[:, None]
    doc_ids = jnp.sum(before.astype(jnp.int32), axis=1)
    begins = jnp.max(jnp.where(before, cuts[None, :], 0), axis=1)
    positions = places - begins
    valid = (places >= 0) & (places < total)
    return (jnp.where(valid, doc_ids, -1), positions)


def rotary(positions):
    half_dim = HD // 2
    inverse = jnp.exp(jnp.arange(half_dim, dtype=F32) * (-2.0 * math.log(THETA) / HD))
    angles = positions.astype(F32)[:, None] * inverse[None, :]
    cosine, sine = jnp.cos(angles), jnp.sin(angles)
    return (
        jnp.concatenate([cosine] * 4, axis=1),
        jnp.concatenate([-sine, sine, -sine, sine], axis=1),
    )


def dot(a, b, dims):
    return lax.dot_general(a, b, (dims, ((), ())), preferred_element_type=F32)


NT = ((1,), (1,))
NN = ((1,), (0,))
TN = ((0,), (0,))


def swap(u):
    lane = lax.broadcasted_iota(jnp.int32, u.shape, 1)
    return jnp.where((lane & 32) == 0, pltpu.roll(u, 96, 1), pltpu.roll(u, 32, 1))


def cut_blocks(rows):
    count = max(rows // LANES, 1)
    return [
        (i * LANES, LANES if i < count - 1 else rows - (count - 1) * LANES) for i in range(count)
    ]


def head_masks(rows):
    lane = lax.broadcasted_iota(jnp.int32, (rows, LANES), 1)
    return ((lane < HD).astype(F32), (lane >= HD).astype(F32))


def load_qkv(rows, q_ref, k_ref, v_ref, c_ref, s_ref):
    cosine, sine = c_ref[...], s_ref[...]
    q = q_ref[0, HALF : HALF + rows, :]
    q = q * cosine[HALF : HALF + rows] + swap(q) * sine[HALF : HALF + rows]
    q = q.astype(BF).astype(F32) * (1.0 / math.sqrt(HD))
    k = k_ref[0]
    k = (k * cosine + swap(k) * sine).astype(BF)
    return q, k, v_ref[0].astype(BF), cosine, sine


def soft(qh, kw, bias):
    scores = dot(qh, kw, NT) + bias
    raised = jnp.exp(scores - jnp.max(scores, axis=1, keepdims=True))
    return raised * (1.0 / jnp.sum(raised, axis=1, keepdims=True))


def fwd_kernel(rows, q_ref, k_ref, v_ref, c_ref, s_ref, b_ref, o_ref):
    q, k, v, _, _ = load_qkv(rows, q_ref, k_ref, v_ref, c_ref, s_ref)
    parts = []
    for start, size in cut_blocks(rows):
        stop = start + size + 2 * HALF
        kw, vw = k[start:stop], v[start:stop]
        bias = b_ref[start : start + size, start:stop]
        masks = head_masks(size)
        total = None
        for mask in masks:
            qh = (q[start : start + size] * mask).astype(BF)
            p = soft(qh, kw, bias)
            part = dot(p.astype(BF), vw, NN) * mask
            total = part if total is None else total + part
        parts.append(total)
    o_ref[0] = jnp.concatenate(parts, axis=0).astype(BF)


def bwd_kernel(rows, q_ref, k_ref, v_ref, c_ref, s_ref, b_ref, g_ref, o_ref, acc):
    which = pl.program_id(1)

    @pl.when(which == 0)
    def _():
        q, k, v, cosine, sine = load_qkv(rows, q_ref, k_ref, v_ref, c_ref, s_ref)
        g = g_ref[0].astype(F32)
        acc[...] = jnp.zeros_like(acc)
        for start, size in cut_blocks(rows):
            stop = start + size + 2 * HALF
            kw, vw = k[start:stop], v[start:stop]
            bias = b_ref[start : start + size, start:stop]
            dq = None
            for mask in head_masks(size):
                qh = (q[start : start + size] * mask).astype(BF)
                gh = (g[start : start + size] * mask).astype(BF)
                p = soft(qh, kw, bias)
                dp = dot(gh, vw, NT)
                centre = jnp.sum(p * dp, axis=1, keepdims=True)
                ds = (p * (dp - centre)).astype(BF)
                part = dot(ds, kw, NN) * (mask * (1.0 / math.sqrt(HD)))
                dq = part if dq is None else dq + part
                acc[1, start:stop, :] += dot(ds, qh, TN)
                acc[2, start:stop, :] += dot(p.astype(BF), gh, TN)
            acc[0, HALF + start : HALF + start + size, :] = dq
        for index in range(2):
            w = acc[index]
            acc[index] = w * cosine - swap(w) * sine

    o_ref[0] = acc[which].astype(BF)


def attention_specs(rows, ext, per):
    def column(j):
        return pl.BlockSpec((1, ext, LANES), lambda i, *_: (i // per, 0, j * per + i % per))

    whole = pl.BlockSpec((ext, LANES), lambda *_: (0, 0))
    bias = pl.BlockSpec((rows, ext), lambda *_: (0, 0))
    return [column(0), column(1), column(2), whole, whole, bias]


def attend_fwd(rows, projected, cosine, sine, bias):
    tp, ext, width = projected.shape
    per = width // 3 // LANES
    return pl.pallas_call(
        lambda *refs: fwd_kernel(rows, *refs),
        grid=(tp * per,),
        in_specs=attention_specs(rows, ext, per),
        out_specs=pl.BlockSpec((1, rows, LANES), lambda i: (i // per, 0, i % per)),
        out_shape=jax.ShapeDtypeStruct((tp, rows, width // 3), BF),
        compiler_params=pltpu.CompilerParams(vmem_limit_bytes=32 * 1024 * 1024),
    )(projected, projected, projected, cosine, sine, bias)


def attend_bwd(rows, projected, cosine, sine, bias, grad):
    tp, ext, width = projected.shape
    per = width // 3 // LANES
    specs = attention_specs(rows, ext, per)
    specs.append(pl.BlockSpec((1, rows, LANES), lambda i, j: (i // per, 0, i % per)))
    return pl.pallas_call(
        lambda *refs: bwd_kernel(rows, *refs),
        grid=(tp * per, 3),
        in_specs=specs,
        out_specs=pl.BlockSpec((1, ext, LANES), lambda i, j: (i // per, 0, j * per + i % per)),
        out_shape=jax.ShapeDtypeStruct((tp, ext, width), BF),
        scratch_shapes=[pltpu.VMEM((3, ext, LANES), F32)],
        compiler_params=pltpu.CompilerParams(vmem_limit_bytes=32 * 1024 * 1024),
    )(projected, projected, projected, cosine, sine, bias, grad)


def pair_kernel(l1_ref, r1_ref, l2_ref, r2_ref, o_ref):
    width = r1_ref.shape[2]
    o_ref[:, :width] = dot(l1_ref[...], r1_ref[0], TN).astype(BF)
    o_ref[:, width:] = dot(l2_ref[...], r2_ref[0], TN).astype(BF)


def pair_products(l1, r1, l2, r2):
    tp, n1, k1 = r1.shape
    n2, k2 = r2.shape[1:]
    deep = l1.shape[1]
    tile = 2 * LANES
    count = deep // tile
    return pl.pallas_call(
        pair_kernel,
        grid=(tp, count),
        in_specs=[
            pl.BlockSpec((n1, tile), lambda t, j: (0, j)),
            pl.BlockSpec((1, n1, k1), lambda t, j: (t, 0, 0)),
            pl.BlockSpec((n2, tile), lambda t, j: (0, j)),
            pl.BlockSpec((1, n2, k2), lambda t, j: (t, 0, 0)),
        ],
        out_specs=pl.BlockSpec((tile, k1 + k2), lambda t, j: (t * count + j, 0)),
        out_shape=jax.ShapeDtypeStruct((tp * deep, k1 + k2), BF),
        compiler_params=pltpu.CompilerParams(vmem_limit_bytes=32 * 1024 * 1024),
    )(l1, r1, l2, r2)


def padded(block):
    return jnp.pad(block, ((0, 0), (0, -block.shape[1] % LANES)))


def total_over_all(value):
    for axis in ROWS:
        count, step = lax.axis_size(axis), 1
        while step < count:
            value = value + lax.ppermute(value, axis, [(i, i ^ step) for i in range(count)])
            step *= 2
    return value


def halving_sum(terms, deep, reverse):
    dp, tp = lax.axis_size("dp"), lax.axis_size("tensor")
    dp_bits, tp_bits = dp.bit_length() - 1, tp.bit_length() - 1
    order = list(range(1, dp_bits))
    steps = [("dp", bit) for bit in [0] + (order[::-1] if reverse else order)]
    steps += [("tensor", bit) for bit in range(tp_bits)]
    dims = [("tensor", bit) for bit in reversed(range(tp_bits))]
    dims += [("dp", bit) for bit in reversed(range(dp_bits))]
    value = terms.reshape([2] * len(dims) + [deep, terms.shape[1]])
    for step in steps:
        name, bit = step
        place = dims.index(step)
        dims.pop(place)
        mine = (lax.axis_index(name) >> bit) & 1
        keep = lax.dynamic_index_in_dim(value, mine, place, keepdims=False)
        send = lax.dynamic_index_in_dim(value, 1 - mine, place, keepdims=False)
        pairs = [(i, i ^ (1 << bit)) for i in range(lax.axis_size(name))]
        got = lax.ppermute(send, name, pairs)
        value = (keep.astype(F32) + got.astype(F32)).astype(BF)
    return value


def ein(spec, a, b):
    return jnp.einsum(spec, a, b, preferred_element_type=F32)


def body(tokens, lengths, gain_attn, w_qkv, w_out, gain_ffn, w_in, w_down, grad_output):
    rows = tokens.shape[0]
    dp, tp = lax.axis_size("dp"), lax.axis_size("tensor")
    devices = dp * tp
    total = rows * devices
    ext = rows + 2 * HALF
    deep = D // dp
    first = lax.axis_index("dp") * deep
    heads_width, units = w_qkv.shape[2], w_in.shape[2]

    blocks = [
        lax.dynamic_slice_in_dim(w_qkv, first, deep, 0).reshape(deep, 3 * heads_width),
        lax.dynamic_slice_in_dim(w_out, first, deep, 1).T,
        lax.dynamic_slice_in_dim(w_in, first, deep, 0).reshape(deep, 2 * units),
        lax.dynamic_slice_in_dim(w_down, first, deep, 1).T,
    ]
    piece = jnp.concatenate([padded(block) for block in blocks], axis=1)
    gathered = lax.all_gather(piece, PIECES, axis=0, tiled=True)
    gathered = with_layout_constraint(gathered, Layout((0, 1))).reshape(tp, D, -1)
    weights, offset = [], 0
    for block in blocks:
        weights.append(gathered[:, :, offset : offset + block.shape[1]])
        offset += block.shape[1] + -block.shape[1] % LANES
    all_qkv, all_out, all_in, all_down = weights

    start = (lax.axis_index("dp") * tp + lax.axis_index("tensor")) * rows
    forward = [(i, i + 1) for i in range(devices - 1)]
    backward = [(i + 1, i) for i in range(devices - 1)]
    x_own = tokens.astype(F32)
    normed_own, norm_pull_one = jax.vjp(layer_norm, x_own, gain_attn)
    normed_low = normed_own.astype(BF)
    normed_ext = jnp.concatenate(
        [
            lax.ppermute(normed_low[rows - HALF :], ROWS, forward),
            normed_low,
            lax.ppermute(normed_low[:HALF], ROWS, backward),
        ],
        axis=0,
    )
    seg_ext, pos_ext = layout(lengths, start - HALF, ext, total)
    cosine, sine = rotary(pos_ext)
    row_ids = jnp.arange(rows, dtype=jnp.int32)[:, None]
    col_ids = jnp.arange(ext, dtype=jnp.int32)[None, :]
    allowed = (jnp.abs(col_ids - HALF - row_ids) <= HALF) & (
        seg_ext[HALF : HALF + rows][:, None] == seg_ext[None, :]
    )
    bias = jnp.where(allowed, 0.0, -1e30).astype(F32)

    projected = ein("nd,tdk->tnk", normed_ext, all_qkv)
    mixed = attend_fwd(rows, projected, cosine, sine, bias)
    residual = x_own + ein("tnc,tdc->nd", mixed, all_out)
    normed_ffn, norm_pull_two = jax.vjp(layer_norm, residual, gain_ffn)
    normed_ffn_low = normed_ffn.astype(BF)
    hidden = ein("nd,tdk->tnk", normed_ffn_low, all_in)

    def gelu_product(values):
        return jax.nn.gelu(values[..., :units], approximate=False) * values[..., units:]

    activated, gelu_pull = jax.vjp(gelu_product, hidden)
    act_low = activated.astype(BF)
    output = (residual + ein("tnf,tdf->nd", act_low, all_down)).astype(BF)

    grad_out32 = grad_output.astype(F32)
    grad_act = ein("nd,tdf->tnf", grad_output, all_down)
    grad_hidden = gelu_pull(grad_act)[0].astype(BF)
    ffn_terms = pair_products(normed_ffn_low, grad_hidden, grad_output, act_low)
    ffn_terms, grad_hidden = lax.optimization_barrier((ffn_terms, grad_hidden))
    ffn_sum = lax.psum_scatter(
        ffn_terms,
        PIECES,
        scatter_dimension=0,
        tiled=True,
    )
    grad_normed_ffn = ein("tnk,tdk->nd", grad_hidden, all_in)
    grad_resid_part, grad_gain_two = norm_pull_two(grad_normed_ffn)
    grad_residual = grad_out32 + grad_resid_part
    grad_res_low = grad_residual.astype(BF)
    grad_mixed = ein("nd,tdc->tnc", grad_res_low, all_out).astype(BF)
    grad_qkv_low = attend_bwd(rows, projected, cosine, sine, bias, grad_mixed)
    attn_terms = pair_products(normed_ext, grad_qkv_low, grad_res_low, mixed)
    middle = attn_terms.shape[1] // 2
    attn_sum = jnp.concatenate(
        [
            halving_sum(attn_terms[:, :middle], deep, False),
            halving_sum(attn_terms[:, middle:], deep, True),
        ],
        axis=1,
    )
    grad_normed_ext = ein("tnk,tdk->nd", grad_qkv_low, all_qkv)
    from_after = lax.ppermute(grad_normed_ext[:HALF].astype(BF), ROWS, backward)
    from_before = lax.ppermute(grad_normed_ext[ext - HALF :].astype(BF), ROWS, forward)
    grad_normed = (
        grad_normed_ext[HALF : HALF + rows]
        + jnp.pad(from_before.astype(F32), ((0, rows - HALF), (0, 0)))
        + jnp.pad(from_after.astype(F32), ((rows - HALF, 0), (0, 0)))
    )
    grad_x_part, grad_gain_one = norm_pull_one(grad_normed)
    grad_tokens = (grad_residual + grad_x_part).astype(BF)
    gains = total_over_all(jnp.stack([grad_gain_one, grad_gain_two]))

    ffn_sum = ffn_sum.astype(F32)
    attn_sum = attn_sum.astype(F32)
    return (
        output,
        grad_tokens,
        gains[0],
        attn_sum[:, : 3 * heads_width].reshape(deep, 3, heads_width),
        attn_sum[:, 3 * heads_width :].T,
        gains[1],
        ffn_sum[:, : 2 * units].reshape(deep, 2, units),
        ffn_sum[:, 2 * units :].T,
    )


def solution(mesh):
    in_specs = (
        P(("dp", "tensor"), None),
        P(),
        P(),
        P(None, None, "tensor"),
        P("tensor", None),
        P(),
        P(None, None, "tensor"),
        P("tensor", None),
        P(("dp", "tensor"), None),
    )
    out_specs = (
        P(("dp", "tensor"), None),
        P(("dp", "tensor"), None),
        P(),
        P("dp", None, "tensor"),
        P("tensor", "dp"),
        P(),
        P("dp", None, "tensor"),
        P("tensor", "dp"),
    )
    return jax.shard_map(body, mesh=mesh, in_specs=in_specs, out_specs=out_specs, check_vma=False)
```
